32 devices in a mesh: tm: 16 (over z, y, x), row: 2 (over core).
Axes of the slice: x: 2, y: 2, z: 4, core: 2. Of those that a mesh axis runs over, the one named last changes fastest.
Arguments:
- trans: bfloat16 [32, 1024, 1024], P('tm', 'row'), may hold values from -0.3 to 0.9
- offset: bfloat16 [32, 1024], P('tm', 'row'), may hold values from -6 to 6
- spread: bfloat16 [32, 1024, 1024], P('tm', 'row'), may hold values from -0.3 to 2.3, as said below
Outputs:
- trans_out: bfloat16 [32, 1024, 1024], P('tm', 'row')
- offset_out: bfloat16 [32, 1024], P('tm', 'row')
- spread_out: bfloat16 [32, 1024, 1024], P('tm', 'row')
The draws below stay inside these ranges and needn't reach their ends.
Inputs may be any that keep to these rules, and one draw needn't show every extreme that they name: `spread`: each block's matrix is symmetric.
All inputs are finite; a program needn't handle non-finite values.
Results may differ from the reference program's by a relative error of at most 0.0056.
Values may be sent and summed in bfloat16 or wider, within the bound.
A program may use at most 64 MiB of HBM per device.

```python
import math
import jax
import jax.numpy as jnp
from jax import lax

D = 1024
LEVELS = 2
BLOCKS = 32


def draw_trans(key, part):
    jitter = jax.random.normal(key, (BLOCKS, D, D), jnp.float32)
    jitter = jnp.clip(jitter, -4.0, 4.0) * (0.5 / math.sqrt(D))
    identity = jnp.eye(D, dtype=jnp.float32)
    return (0.6 * identity[None] + jitter).astype(jnp.bfloat16)


def draw_spread(key, part):
    matrix = jax.random.normal(jax.random.fold_in(key, 1), (BLOCKS, D, D), jnp.float32)
    matrix = jnp.clip(matrix, -4.0, 4.0) * (0.5 / math.sqrt(D))
    symmetric = 0.5 * (matrix + jnp.swapaxes(matrix, 1, 2))
    diagonal = jnp.exp(jax.random.uniform(jax.random.fold_in(key, 2), (BLOCKS, D), jnp.float32, math.log(0.5), math.log(2.0)))
    identity = jnp.eye(D, dtype=jnp.float32)
    return (symmetric + diagonal[:, :, None] * identity[None]).astype(jnp.bfloat16)


def levels(own_key, extent, split, least, high):
    factor_of, own = 1.0, jax.random.fold_in(own_key, 6)
    for position, blocks in split:
        heights = jnp.exp(jax.random.uniform(jax.random.fold_in(own, position), (blocks,), jnp.float32, least / len(split), high / len(split)))
        factor_of = factor_of * jnp.repeat(heights, extent[position] // blocks).reshape([-1 if axis == position else 1 for axis in range(len(extent))])
    return factor_of


def normal_values(rng, shape, scale, most, pieces=(), kind=jnp.bfloat16):
    entries = jax.random.normal(rng, shape, jnp.float32) * scale
    if len(pieces) > 0:
        entries = levels(rng, shape, pieces, -0.22, 0.18) * entries
    return jnp.clip(entries, min=-most, max=most).astype(kind)


def setup_inputs(seed: int = 0) -> dict:
    arg_keys = jax.random.split(jax.random.key(seed), 4)
    return {
        "trans": draw_trans(jax.random.fold_in(arg_keys[3], 71), 0),
        "offset": normal_values(arg_keys[1], (BLOCKS, D), 1.0, 6.0, ((0, 16), (1, 2))),
        "spread": draw_spread(jax.random.fold_in(arg_keys[3], 71), 0),
    }


def compose(left_trans, left_offset, left_spread, right_trans, right_offset, right_spread):
    trans_left = left_trans.astype(jnp.float32)
    trans_right = right_trans.astype(jnp.float32)
    new_trans = jnp.einsum("bik,bkj->bij", trans_left, trans_right).astype(jnp.bfloat16)
    new_offset = (jnp.einsum("bik,bk->bi", trans_left, right_offset.astype(jnp.float32)) + left_offset.astype(jnp.float32)).astype(jnp.bfloat16)
    partial_value = jnp.einsum("bik,bkj->bij", trans_left, right_spread.astype(jnp.float32))
    partial_value = lax.optimization_barrier(partial_value.astype(jnp.bfloat16)).astype(jnp.float32)
    new_spread = (jnp.einsum("bik,bjk->bij", partial_value, trans_left) + left_spread.astype(jnp.float32)).astype(jnp.bfloat16)
    return new_trans, new_offset, new_spread


def reference(trans, offset, spread):
    for doubling in range(LEVELS):
        stride = 2 ** doubling
        leading = BLOCKS - stride
        merged = compose(trans[:leading], offset[:leading], spread[:leading], trans[stride:], offset[stride:], spread[stride:])
        trans = jnp.concatenate([merged[0], trans[leading:]], axis=0)
        offset = jnp.concatenate([merged[1], offset[leading:]], axis=0)
        spread = jnp.concatenate([merged[2], spread[leading:]], axis=0)
    return trans, offset, spread
```

```python
import jax
import jax.numpy as jnp
from jax import lax
from jax.sharding import PartitionSpec as P


def from_later(block, distance):
    devices = range(lax.axis_size("tm"))
    route = [(i, i - distance) for i in devices if i - distance in devices]
    return lax.ppermute(block, "tm", route)


def rows_of_all(block):
    return lax.all_gather(block, "row", axis=0, tiled=True)


def product(a, b):
    return jnp.dot(a, b, preferred_element_type=jnp.float32)


def compose(own, own_trans_full, later_full):
    trans, offset, spread = own
    far_trans, far_offset, far_spread = later_full
    mixed_trans = product(trans, far_trans).astype(jnp.bfloat16)
    mixed_offset = (product(trans, far_offset) + offset.astype(jnp.float32)).astype(jnp.bfloat16)
    partial_value = product(trans, far_spread).astype(jnp.bfloat16)
    mixed_spread = jnp.einsum("ik,jk->ij", partial_value, own_trans_full, preferred_element_type=jnp.float32)
    mixed_spread = (mixed_spread + spread.astype(jnp.float32)).astype(jnp.bfloat16)
    return mixed_trans, mixed_offset, mixed_spread


def on_device(trans, offset, spread):
    count = lax.axis_size("tm")
    position = lax.axis_index("tm")
    zero = (trans[0], offset[0], spread[0])
    one = (trans[1], offset[1], spread[1])
    four = from_later(zero, 2)
    one_full = tuple(rows_of_all(x) for x in one)
    zero_trans_full = rows_of_all(trans[0])
    pair = compose(zero, zero_trans_full, one_full)
    next_pair = from_later(pair, 1)
    four_full = tuple(rows_of_all(x) for x in four)
    pair_trans_full = rows_of_all(pair[0])
    next_full = tuple(rows_of_all(x) for x in next_pair)
    triple = compose(one, one_full[0], next_full)
    triple_trans_full = rows_of_all(triple[0])
    first = compose(pair, pair_trans_full, next_full)
    second = compose(triple, triple_trans_full, four_full)
    is_last = position == count - 1
    is_before = position == count - 2
    first = tuple(jnp.where(is_last, a, b) for a, b in zip(pair, first))
    second = tuple(jnp.where(is_last, a, jnp.where(is_before, b, c)) for a, b, c in zip(one, triple, second))
    return tuple(jnp.stack([a, b]) for a, b in zip(first, second))


def solution(mesh):
    placed = (P("tm", "row", None), P("tm", "row"), P("tm", "row", None))
    return jax.shard_map(on_device, mesh=mesh, in_specs=placed, out_specs=placed, check_vma=False)
```

```python
import functools
import jax
import jax.numpy as jnp
from jax import lax
from jax.experimental import pallas as pl
from jax.experimental.pallas import tpu as pltpu
from jax.sharding import PartitionSpec as P

MESH = pl.DeviceIdType.MESH
LINES = 16
TILE = 256


def pieces(core, cores, rows, width):
    if cores != 2 or rows % 256 or width != 2 * rows:
        return [(0, rows, 0, width)]
    q = rows // 2
    return [
        (0, q, core * (2 * q), 2 * q),
        (core * q, q, (2 + core) * q, q),
        (q, q, (1 - core) * q, 2 * q),
    ]


def mirror(matrix, cores, rows, width):
    if cores != 2 or rows % 256 or width != 2 * rows:
        return
    q = rows // 2
    for i, j in ((1, 0), (2, 0), (2, 1), (3, 2), (0, 3), (1, 3)):
        block = matrix[pl.ds(j * q, q), pl.ds(i * q, q)]
        matrix[pl.ds(i * q, q), pl.ds(j * q, q)] = block.T


def kernel(
    count, cores, trans, goff, spread, out_trans, out_goff, out_spread,
    e0, e1, l1, pe, ne, nl, fe, fl, te, mixed, pl_own, tl_own, g1, ng, fg, pg, tg,
    send_sem, recv_sem,
):
    rows, width = trans.shape[1:]
    tile = min(TILE, width)
    position = lax.axis_index("tm")
    core = lax.axis_index("row")
    peers = [(k, lax.rem(core + k, cores)) for k in range(1, cores)]
    used = [0]

    barrier = pltpu.get_barrier_semaphore()
    expected = jnp.int32(cores - 1)
    for _, peer in peers:
        pl.semaphore_signal(barrier, inc=1, device_id={"row": peer}, device_id_type=MESH)
    for step in (-2, -1, 1, 2):
        there = jnp.logical_and(position + step >= 0, position + step < count)
        expected = expected + there.astype(jnp.int32)

        @pl.when(there)
        def _(step=step):
            pl.semaphore_signal(barrier, inc=1, device_id={"tm": position + step}, device_id_type=MESH)

    pl.semaphore_wait(barrier, expected)

    def remote(source, target, device):
        k = used[0]
        used[0] += 1
        return pltpu.make_async_remote_copy(
            src_ref=source, dst_ref=target, send_sem=send_sem.at[k], recv_sem=recv_sem.at[k],
            device_id=device, device_id_type=MESH,
        )

    def place(index, size):
        if isinstance(index, int):
            return pl.ds(index, size)
        return pl.ds(pl.multiple_of(index, 128), size)

    own = place(core * rows, rows)

    def spread_rows(matrix, parts, source=None):
        copies = []
        for row, n_rows, column, n_columns in parts:
            target = matrix.at[place(core * rows + row, n_rows), place(column, n_columns)]
            if source is None:
                origin = target
            else:
                origin = source.at[place(row, n_rows), place(column, n_columns)]
            copies.append((origin, target))
        return copies

    whole = [(0, rows, 0, width)]
    half = pieces(core, cores, rows, width)

    def to_device(pairs, device):
        return [remote(a, b, device) for a, b in pairs]

    def to_peers(pairs):
        return [remote(a, b, {"row": peer}) for _, peer in peers for a, b in pairs]

    def start(copies):
        for copy in copies:
            copy.start()

    def arrived(copies):
        for copy in copies:
            copy.wait_recv()

    def left(copies):
        for copy in copies:
            copy.wait_send()

    def times(a, b, out):
        @pl.loop(0, width // tile)
        def _(n):
            columns = pl.ds(pl.multiple_of(n * tile, tile), tile)
            out[:, columns] = jnp.dot(
                a[...], b[:, columns], preferred_element_type=jnp.float32
            ).astype(jnp.bfloat16)

    def times_transposed(a, b, added, out):
        @pl.loop(0, width // tile)
        def _(n):
            columns = pl.ds(pl.multiple_of(n * tile, tile), tile)
            value = lax.dot_general(
                a[...], b[columns, :], (((1,), (1,)), ((), ())), preferred_element_type=jnp.float32
            )
            out[:, columns] = (value + added[:, columns].astype(jnp.float32)).astype(jnp.bfloat16)

    def shift(a, g, added, out):
        total = added[...].astype(jnp.float32)
        for k in range(cores):
            total = total + lax.dot_general(
                g[k], a[:, pl.ds(k * rows, rows)], (((1,), (1,)), ((), ())),
                preferred_element_type=jnp.float32,
            )
        out[...] = total.astype(jnp.bfloat16)

    two = {"tm": position - 2}
    one = {"tm": position - 1}
    row_e1 = to_peers(spread_rows(e1, whole, trans.at[1]))
    row_l1 = to_peers(spread_rows(l1, whole, spread.at[1]))
    row_g1 = to_peers([(goff.at[1], g1.at[core])])
    row_e0 = to_peers(spread_rows(e0, whole, trans.at[0]))
    far_e = to_device(spread_rows(fe, whole, trans.at[0]), two)
    far_l = to_device(spread_rows(fl, half, spread.at[0]), two)
    far_g = to_device([(goff.at[0], fg.at[core])], two)
    next_e = to_device(spread_rows(ne, whole, pe.at[own, :]), one)
    next_l = to_device(spread_rows(nl, half, pl_own), one)
    next_g = to_device([(pg, ng.at[core])], one)
    row_pe = to_peers(spread_rows(pe, whole))
    row_fe = to_peers(spread_rows(fe, whole))
    row_fl = to_peers(spread_rows(fl, half))
    row_fg = to_peers([(fg.at[core], fg.at[core])])
    row_ne = to_peers(spread_rows(ne, whole))
    row_nl = to_peers(spread_rows(nl, half))
    row_ng = to_peers([(ng.at[core], ng.at[core])])
    row_te = to_peers(spread_rows(te, whole))

    gives_two = position >= 2
    gives_one = position >= 1
    takes_two = position + 2 < count
    takes_one = position + 1 < count

    start(row_e1)

    @pl.when(gives_two)
    def _():
        start(far_e + far_g + far_l)

    start(row_g1 + row_l1 + row_e0)
    e1[own, :] = trans[1]
    l1[own, :] = spread[1]
    e0[own, :] = trans[0]
    g1[core] = goff[1]

    arrived(row_e1)
    times(trans.at[0], e1, pe.at[own, :])
    start(row_pe)

    @pl.when(gives_one)
    def _():
        start(next_e)

    arrived(row_g1)
    shift(trans.at[0], g1, goff.at[0], pg)
    arrived(row_l1)
    times(trans.at[0], l1, mixed)
    arrived(row_e0)
    times_transposed(mixed, e0, spread.at[0], pl_own)

    @pl.when(gives_one)
    def _():
        start(next_g + next_l)

    arrived(row_pe)

    @pl.when(takes_two)
    def _():
        arrived(far_e)
        start(row_fe)
        arrived(far_g)
        start(row_fg)

    @pl.when(takes_one)
    def _():
        arrived(next_e)
        start(row_ne)
        arrived(next_g)
        start(row_ng)
        arrived(row_ne)
        times(trans.at[1], ne, te.at[own, :])
        start(row_te)
        times(pe.at[own, :], ne, out_trans.at[0])
        arrived(row_ng)
        shift(trans.at[1], ng, goff.at[1], tg)
        shift(pe.at[own, :], ng, pg, out_goff.at[0])

    @pl.when(takes_two)
    def _():
        arrived(far_l)
        start(row_fl)
        arrived(row_fe)
        times(te.at[own, :], fe, out_trans.at[1])
        arrived(row_fg)
        shift(te.at[own, :], fg, tg, out_goff.at[1])
        arrived(row_fl)
        mirror(fl, cores, rows, width)

    @pl.when(takes_one)
    def _():
        arrived(next_l)
        start(row_nl)
        arrived(row_nl)
        mirror(nl, cores, rows, width)
        times(pe.at[own, :], nl, mixed)
        times_transposed(mixed, pe, pl_own, out_spread.at[0])
        times(trans.at[1], nl, mixed)
        times_transposed(mixed, e1, spread.at[1], tl_own)
        arrived(row_te)

    @pl.when(takes_two)
    def _():
        times(te.at[own, :], fl, mixed)
        times_transposed(mixed, te, tl_own, out_spread.at[1])

    @pl.when(position == count - 2)
    def _():
        out_trans[1] = te[own, :]
        out_spread[1] = tl_own[...]
        out_goff[1] = tg[...]

    @pl.when(position == count - 1)
    def _():
        out_trans[0] = pe[own, :]
        out_spread[0] = pl_own[...]
        out_goff[0] = pg[...]
        out_trans[1] = trans[1]
        out_spread[1] = spread[1]
        out_goff[1] = goff[1]

    left(row_e1 + row_l1 + row_g1 + row_e0 + row_pe)

    @pl.when(gives_two)
    def _():
        left(far_e + far_g + far_l)

    @pl.when(gives_one)
    def _():
        left(next_e + next_g + next_l)

    @pl.when(takes_two)
    def _():
        left(row_fe + row_fg + row_fl)

    @pl.when(takes_one)
    def _():
        left(row_ne + row_ng + row_nl + row_te)


def on_device(count, cores, trans, offset, spread):
    _, rows, width = trans.shape
    kind = trans.dtype
    goff = jnp.broadcast_to(offset[:, None, :], (2, LINES, rows))
    full = pltpu.VMEM((width, width), kind)
    part = pltpu.VMEM((rows, width), kind)
    lines = pltpu.VMEM((cores, LINES, rows), kind)
    line = pltpu.VMEM((LINES, rows), kind)
    n_copies = 10 + 20 * (cores - 1)
    vmem = pl.BlockSpec(memory_space=pltpu.VMEM)
    flops = 12 * 2 * rows * width * width
    a, b, c = pl.pallas_call(
        functools.partial(kernel, count, cores),
        out_shape=(
            jax.ShapeDtypeStruct(trans.shape, kind),
            jax.ShapeDtypeStruct(goff.shape, kind),
            jax.ShapeDtypeStruct(spread.shape, kind),
        ),
        in_specs=[vmem] * 3,
        out_specs=(vmem,) * 3,
        scratch_shapes=[full] * 9 + [part] * 3 + [lines] * 3 + [line] * 2
        + [pltpu.SemaphoreType.DMA((n_copies,)), pltpu.SemaphoreType.DMA((n_copies,))],
        compiler_params=pltpu.CompilerParams(
            collective_id=0, has_side_effects=True, vmem_limit_bytes=56 * 1024 * 1024
        ),
        cost_estimate=pl.CostEstimate(flops=flops, bytes_accessed=4 * trans.size * 2, transcendentals=0),
    )(trans, goff, spread)
    return a, b[:, 0, :], c


def solution(mesh):
    placed = (P("tm", "row", None), P("tm", "row"), P("tm", "row", None))
    body = functools.partial(on_device, mesh.shape["tm"], mesh.shape["row"])
    return jax.shard_map(body, mesh=mesh, in_specs=placed, out_specs=placed, check_vma=False)
```

```python
import functools
import jax
import jax.numpy as jnp
from jax import lax
from jax.experimental import pallas as pl
from jax.experimental.pallas import tpu as pltpu
from jax.sharding import PartitionSpec as P

MESH = pl.DeviceIdType.MESH
LINES = 16
TILE = 256


def pieces(core, cores, rows, width):
    if cores != 2 or rows % 256 or width != 2 * rows:
        return [(0, rows, 0, width)]
    q = rows // 2
    return [
        (0, q, core * (2 * q), 2 * q),
        (core * q, q, (2 + core) * q, q),
        (q, q, (1 - core) * q, 2 * q),
    ]


def mirror(matrix, cores, rows, width):
    if cores != 2 or rows % 256 or width != 2 * rows:
        return
    q = rows // 2
    for i, j in ((1, 0), (2, 0), (2, 1), (3, 2), (0, 3), (1, 3)):
        block = matrix[pl.ds(j * q, q), pl.ds(i * q, q)]
        matrix[pl.ds(i * q, q), pl.ds(j * q, q)] = block.T


def kernel(
    count, cores, trans, goff, spread, out_trans, out_goff, out_spread,
    e0, e1, l1, pe, ne, nl, fe, fl, te, mixed, mixed_far, relay, pl_own, tl_own, g1, ng, fg, pg, tg,
    send_sem, recv_sem,
):
    rows, width = trans.shape[1:]
    tile = min(TILE, width)
    position = lax.axis_index("tm")
    core = lax.axis_index("row")
    peers = [(k, lax.rem(core + k, cores)) for k in range(1, cores)]
    used = [0]

    barrier = pltpu.get_barrier_semaphore()
    expected = jnp.int32(cores - 1)
    for _, peer in peers:
        pl.semaphore_signal(barrier, inc=1, device_id={"row": peer}, device_id_type=MESH)
    for step in (-2, -1, 1, 2):
        there = jnp.logical_and(position + step >= 0, position + step < count)
        expected = expected + there.astype(jnp.int32)

        @pl.when(there)
        def _(step=step):
            pl.semaphore_signal(barrier, inc=1, device_id={"tm": position + step}, device_id_type=MESH)

    pl.semaphore_wait(barrier, expected)

    def remote(source, target, device):
        k = used[0]
        used[0] += 1
        return pltpu.make_async_remote_copy(
            src_ref=source, dst_ref=target, send_sem=send_sem.at[k], recv_sem=recv_sem.at[k],
            device_id=device, device_id_type=MESH,
        )

    def place(index, size):
        if isinstance(index, int):
            return pl.ds(index, size)
        return pl.ds(pl.multiple_of(index, 128), size)

    own = place(core * rows, rows)

    def spread_rows(matrix, parts, source=None):
        copies = []
        for row, n_rows, column, n_columns in parts:
            target = matrix.at[place(core * rows + row, n_rows), place(column, n_columns)]
            if source is None:
                origin = target
            else:
                origin = source.at[place(row, n_rows), place(column, n_columns)]
            copies.append((origin, target))
        return copies

    whole = [(0, rows, 0, width)]
    half = pieces(core, cores, rows, width)

    def to_device(pairs, device):
        return [remote(a, b, device) for a, b in pairs]

    def to_peers(pairs):
        return [remote(a, b, {"row": peer}) for _, peer in peers for a, b in pairs]

    def start(copies):
        for copy in copies:
            copy.start()

    def arrived(copies):
        for copy in copies:
            copy.wait_recv()

    def left(copies):
        for copy in copies:
            copy.wait_send()

    def times(a, b, out):
        @pl.loop(0, width // tile)
        def _(n):
            columns = pl.ds(pl.multiple_of(n * tile, tile), tile)
            out[:, columns] = jnp.dot(
                a[...], b[:, columns], preferred_element_type=jnp.float32
            ).astype(jnp.bfloat16)

    def times_transposed(a, b, added, out):
        @pl.loop(0, width // tile)
        def _(n):
            columns = pl.ds(pl.multiple_of(n * tile, tile), tile)
            value = lax.dot_general(
                a[...], b[columns, :], (((1,), (1,)), ((), ())), preferred_element_type=jnp.float32
            )
            out[:, columns] = (value + added[:, columns].astype(jnp.float32)).astype(jnp.bfloat16)

    def shift(a, g, added, out):
        total = added[...].astype(jnp.float32)
        for k in range(cores):
            total = total + lax.dot_general(
                g[k], a[:, pl.ds(k * rows, rows)], (((1,), (1,)), ((), ())),
                preferred_element_type=jnp.float32,
            )
        out[...] = total.astype(jnp.bfloat16)

    two = {"tm": position - 2}
    one = {"tm": position - 1}
    row_e1 = to_peers(spread_rows(e1, whole, trans.at[1]))
    row_l1 = to_peers(spread_rows(l1, whole, spread.at[1]))
    row_g1 = to_peers([(goff.at[1], g1.at[core])])
    row_e0 = to_peers(spread_rows(e0, whole, trans.at[0]))
    far_e = to_device(spread_rows(fe, whole, trans.at[0]), two)
    far_l = to_device(spread_rows(fl, half, spread.at[0]), two)
    far_g = to_device([(goff.at[0], fg.at[core])], two)
    next_e = to_device(spread_rows(ne, whole, pe.at[own, :]), one)
    next_l = to_device(spread_rows(nl, half, pl_own), one)
    relay_l = to_device(
        [(pl_own.at[place(a, n), place(b, m)], relay.at[place(a, n), place(b, m)]) for a, n, b, m in half], two
    )
    forward_l = to_device(spread_rows(nl, half, relay), {"tm": position + 1})
    next_g = to_device([(pg, ng.at[core])], one)
    row_pe = to_peers(spread_rows(pe, whole))
    row_fe = to_peers(spread_rows(fe, whole))
    row_fl = to_peers(spread_rows(fl, half))
    row_fg = to_peers([(fg.at[core], fg.at[core])])
    row_ne = to_peers(spread_rows(ne, whole))
    row_nl = to_peers(spread_rows(nl, half))
    row_ng = to_peers([(ng.at[core], ng.at[core])])
    row_te = to_peers(spread_rows(te, whole))

    gives_two = position >= 2
    gives_one = position >= 1
    takes_two = position + 2 < count
    takes_one = position + 1 < count
    even = lax.rem(position, 2) == 0
    gives_direct = jnp.logical_and(gives_one, jnp.logical_not(even))
    gives_relay = jnp.logical_and(gives_one, even)
    forwards = jnp.logical_and(takes_two, even)
    takes_direct = jnp.logical_and(takes_one, even)
    takes_forward = jnp.logical_and(takes_one, jnp.logical_not(even))

    start(row_e1)

    @pl.when(gives_two)
    def _():
        start(far_e + far_g + far_l)

    start(row_g1 + row_l1 + row_e0)
    e1[own, :] = trans[1]
    l1[own, :] = spread[1]
    e0[own, :] = trans[0]
    g1[core] = goff[1]

    arrived(row_e1)
    times(trans.at[0], e1, pe.at[own, :])
    start(row_pe)

    @pl.when(gives_one)
    def _():
        start(next_e)

    arrived(row_g1)
    shift(trans.at[0], g1, goff.at[0], pg)
    arrived(row_l1)
    times(trans.at[0], l1, mixed)
    arrived(row_e0)
    times_transposed(mixed, e0, spread.at[0], pl_own)

    @pl.when(gives_one)
    def _():
        start(next_g)

    @pl.when(gives_direct)
    def _():
        start(next_l)

    @pl.when(gives_relay)
    def _():
        start(relay_l)

    arrived(row_pe)

    @pl.when(takes_two)
    def _():
        arrived(far_e)
        start(row_fe)
        arrived(far_g)
        start(row_fg)

    @pl.when(takes_one)
    def _():
        arrived(next_e)
        start(row_ne)
        arrived(next_g)
        start(row_ng)
        arrived(row_ne)
        times(trans.at[1], ne, te.at[own, :])
        start(row_te)
        times(pe.at[own, :], ne, out_trans.at[0])
        arrived(row_ng)
        shift(trans.at[1], ng, goff.at[1], tg)
        shift(pe.at[own, :], ng, pg, out_goff.at[0])

    @pl.when(takes_two)
    def _():
        arrived(far_l)
        start(row_fl)

    @pl.when(forwards)
    def _():
        for copy, onward in zip(relay_l, forward_l):
            copy.wait_recv()
            onward.start()

    @pl.when(takes_two)
    def _():
        arrived(row_fe)
        times(te.at[own, :], fe, out_trans.at[1])
        arrived(row_fg)
        shift(te.at[own, :], fg, tg, out_goff.at[1])
        arrived(row_fl)
        mirror(fl, cores, rows, width)
        times(te.at[own, :], fl, mixed_far)

    @pl.when(takes_direct)
    def _():
        for copy, onward in zip(next_l, row_nl):
            copy.wait_recv()
            onward.start()

    @pl.when(takes_forward)
    def _():
        for copy, onward in zip(forward_l, row_nl):
            copy.wait_recv()
            onward.start()

    @pl.when(takes_one)
    def _():
        start(row_nl[len(half):])
        arrived(row_nl)
        mirror(nl, cores, rows, width)
        times(pe.at[own, :], nl, mixed)
        times_transposed(mixed, pe, pl_own, out_spread.at[0])
        times(trans.at[1], nl, mixed)
        times_transposed(mixed, e1, spread.at[1], tl_own)
        arrived(row_te)

    @pl.when(takes_two)
    def _():
        times_transposed(mixed_far, te, tl_own, out_spread.at[1])

    @pl.when(position == count - 2)
    def _():
        out_trans[1] = te[own, :]
        out_spread[1] = tl_own[...]
        out_goff[1] = tg[...]

    @pl.when(position == count - 1)
    def _():
        out_trans[0] = pe[own, :]
        out_spread[0] = pl_own[...]
        out_goff[0] = pg[...]
        out_trans[1] = trans[1]
        out_spread[1] = spread[1]
        out_goff[1] = goff[1]

    left(row_e1 + row_l1 + row_g1 + row_e0 + row_pe)

    @pl.when(gives_two)
    def _():
        left(far_e + far_g + far_l)

    @pl.when(gives_one)
    def _():
        left(next_e + next_g)

    @pl.when(gives_direct)
    def _():
        left(next_l)

    @pl.when(gives_relay)
    def _():
        left(relay_l)

    @pl.when(forwards)
    def _():
        left(forward_l)

    @pl.when(takes_two)
    def _():
        left(row_fe + row_fg + row_fl)

    @pl.when(takes_one)
    def _():
        left(row_ne + row_ng + row_nl + row_te)


def on_device(count, cores, trans, offset, spread):
    _, rows, width = trans.shape
    kind = trans.dtype
    goff = jnp.broadcast_to(offset[:, None, :], (2, LINES, rows))
    full = pltpu.VMEM((width, width), kind)
    part = pltpu.VMEM((rows, width), kind)
    lines = pltpu.VMEM((cores, LINES, rows), kind)
    line = pltpu.VMEM((LINES, rows), kind)
    n_copies = 20 + 20 * (cores - 1)
    vmem = pl.BlockSpec(memory_space=pltpu.VMEM)
    flops = 12 * 2 * rows * width * width
    a, b, c = pl.pallas_call(
        functools.partial(kernel, count, cores),
        out_shape=(
            jax.ShapeDtypeStruct(trans.shape, kind),
            jax.ShapeDtypeStruct(goff.shape, kind),
            jax.ShapeDtypeStruct(spread.shape, kind),
        ),
        in_specs=[vmem] * 3,
        out_specs=(vmem,) * 3,
        scratch_shapes=[full] * 9 + [part] * 5 + [lines] * 3 + [line] * 2
        + [pltpu.SemaphoreType.DMA((n_copies,)), pltpu.SemaphoreType.DMA((n_copies,))],
        compiler_params=pltpu.CompilerParams(
            collective_id=0, has_side_effects=True, vmem_limit_bytes=56 * 1024 * 1024
        ),
        cost_estimate=pl.CostEstimate(flops=flops, bytes_accessed=4 * trans.size * 2, transcendentals=0),
    )(trans, goff, spread)
    return a, b[:, 0, :], c


def solution(mesh):
    placed = (P("tm", "row", None), P("tm", "row"), P("tm", "row", None))
    body = functools.partial(on_device, mesh.shape["tm"], mesh.shape["row"])
    return jax.shard_map(body, mesh=mesh, in_specs=placed, out_specs=placed, check_vma=False)
```

```python
import functools
import jax
import jax.numpy as jnp
from jax import lax
from jax.experimental import pallas as pl
from jax.experimental.pallas import tpu as pltpu
from jax.sharding import PartitionSpec as P

MESH = pl.DeviceIdType.MESH
LINES = 16
TILE = 256


def pieces(core, cores, rows, width):
    if cores != 2 or rows % 256 or width != 2 * rows:
        return [(0, rows, 0, width)]
    q = rows // 2
    return [
        (0, q, core * (2 * q), 2 * q),
        (core * q, q, (2 + core) * q, q),
        (q, q, (1 - core) * q, 2 * q),
    ]


def mirror(matrix, cores, rows, width):
    if cores != 2 or rows % 256 or width != 2 * rows:
        return
    q = rows // 2
    for i, j in ((1, 0), (2, 0), (2, 1), (3, 2), (0, 3), (1, 3)):
        block = matrix[pl.ds(j * q, q), pl.ds(i * q, q)]
        matrix[pl.ds(i * q, q), pl.ds(j * q, q)] = block.T


def kernel(
    count, cores, trans, goff, spread, out_trans, out_goff, out_spread,
    e0, e1, l1, pe, ne, nl, fe, fl, te, mixed, mixed_far, relay, pl_own, tl_own, g1, ng, fg, pg, tg,
    send_sem, recv_sem,
):
    rows, width = trans.shape[1:]
    tile = min(TILE, width)
    position = lax.axis_index("tm")
    core = lax.axis_index("row")
    peers = [(k, lax.rem(core + k, cores)) for k in range(1, cores)]
    used = [0]

    barrier = pltpu.get_barrier_semaphore()
    expected = jnp.int32(cores - 1)
    for _, peer in peers:
        pl.semaphore_signal(barrier, inc=1, device_id={"row": peer}, device_id_type=MESH)
    quads = count % 4 == 0
    quarter = lax.rem(position, 4)
    for step in (-2, -1, 1, 2) + ((-3, 3) if quads else ()):
        there = jnp.logical_and(position + step >= 0, position + step < count)
        if step == -3:
            there = jnp.logical_and(there, quarter == 2)
        if step == 3:
            there = jnp.logical_and(there, quarter == 3)
        expected = expected + there.astype(jnp.int32)

        @pl.when(there)
        def _(step=step):
            pl.semaphore_signal(barrier, inc=1, device_id={"tm": position + step}, device_id_type=MESH)

    pl.semaphore_wait(barrier, expected)

    def remote(source, target, device):
        k = used[0]
        used[0] += 1
        return pltpu.make_async_remote_copy(
            src_ref=source, dst_ref=target, send_sem=send_sem.at[k], recv_sem=recv_sem.at[k],
            device_id=device, device_id_type=MESH,
        )

    def place(index, size):
        if isinstance(index, int):
            return pl.ds(index, size)
        return pl.ds(pl.multiple_of(index, 128), size)

    own = place(core * rows, rows)

    def spread_rows(matrix, parts, source=None):
        copies = []
        for row, n_rows, column, n_columns in parts:
            target = matrix.at[place(core * rows + row, n_rows), place(column, n_columns)]
            if source is None:
                origin = target
            else:
                origin = source.at[place(row, n_rows), place(column, n_columns)]
            copies.append((origin, target))
        return copies

    whole = [(0, rows, 0, width)]
    half = pieces(core, cores, rows, width)

    def to_device(pairs, device):
        return [remote(a, b, device) for a, b in pairs]

    def to_peers(pairs):
        return [remote(a, b, {"row": peer}) for _, peer in peers for a, b in pairs]

    def start(copies):
        for copy in copies:
            copy.start()

    def arrived(copies):
        for copy in copies:
            copy.wait_recv()

    def left(copies):
        for copy in copies:
            copy.wait_send()

    def times(a, b, out):
        @pl.loop(0, width // tile)
        def _(n):
            columns = pl.ds(pl.multiple_of(n * tile, tile), tile)
            out[:, columns] = jnp.dot(
                a[...], b[:, columns], preferred_element_type=jnp.float32
            ).astype(jnp.bfloat16)

    def times_transposed(a, b, added, out):
        @pl.loop(0, width // tile)
        def _(n):
            columns = pl.ds(pl.multiple_of(n * tile, tile), tile)
            value = lax.dot_general(
                a[...], b[columns, :], (((1,), (1,)), ((), ())), preferred_element_type=jnp.float32
            )
            out[:, columns] = (value + added[:, columns].astype(jnp.float32)).astype(jnp.bfloat16)

    def shift(a, g, added, out):
        total = added[...].astype(jnp.float32)
        for k in range(cores):
            total = total + lax.dot_general(
                g[k], a[:, pl.ds(k * rows, rows)], (((1,), (1,)), ((), ())),
                preferred_element_type=jnp.float32,
            )
        out[...] = total.astype(jnp.bfloat16)

    two = {"tm": position - 2}
    relay_at, forward_to = position - 2, position + 1
    if quads:
        relay_at = jnp.where(quarter == 0, position + 2, position - 2)
        forward_to = jnp.where(quarter == 0, position + 1, position - 3)
    one = {"tm": position - 1}
    row_e1 = to_peers(spread_rows(e1, whole, trans.at[1]))
    row_l1 = to_peers(spread_rows(l1, whole, spread.at[1]))
    row_g1 = to_peers([(goff.at[1], g1.at[core])])
    row_e0 = to_peers(spread_rows(e0, whole, trans.at[0]))
    far_e = to_device(spread_rows(fe, whole, trans.at[0]), two)
    far_l = to_device(spread_rows(fl, half, spread.at[0]), two)
    far_g = to_device([(goff.at[0], fg.at[core])], two)
    next_e = to_device(spread_rows(ne, whole, pe.at[own, :]), one)
    next_l = to_device(spread_rows(nl, half, pl_own), one)
    relay_l = to_device(
        [(pl_own.at[place(a, n), place(b, m)], relay.at[place(a, n), place(b, m)]) for a, n, b, m in half],
        {"tm": relay_at},
    )
    forward_l = to_device(spread_rows(nl, half, relay), {"tm": forward_to})
    next_g = to_device([(pg, ng.at[core])], one)
    row_pe = to_peers(spread_rows(pe, whole))
    row_fe = to_peers(spread_rows(fe, whole))
    row_fl = to_peers(spread_rows(fl, half))
    row_fg = to_peers([(fg.at[core], fg.at[core])])
    row_ne = to_peers(spread_rows(ne, whole))
    row_nl = to_peers(spread_rows(nl, half))
    row_ng = to_peers([(ng.at[core], ng.at[core])])
    row_te = to_peers(spread_rows(te, whole))

    gives_two = position >= 2
    gives_one = position >= 1
    takes_two = position + 2 < count
    takes_one = position + 1 < count
    even = lax.rem(position, 2) == 0
    gives_direct = jnp.logical_and(gives_one, jnp.logical_not(even))
    gives_relay = jnp.logical_and(gives_one, even)
    forwards = jnp.logical_and(takes_two, even)
    if quads:
        forwards = jnp.logical_or(quarter == 0, jnp.logical_and(quarter == 2, position > 2))
    takes_direct = jnp.logical_and(takes_one, even)
    takes_forward = jnp.logical_and(takes_one, jnp.logical_not(even))

    start(row_e1)

    @pl.when(gives_two)
    def _():
        start(far_e + far_g + far_l)

    start(row_g1 + row_l1 + row_e0)
    e1[own, :] = trans[1]
    l1[own, :] = spread[1]
    e0[own, :] = trans[0]
    g1[core] = goff[1]

    arrived(row_e1)
    times(trans.at[0], e1, pe.at[own, :])
    start(row_pe)

    @pl.when(gives_one)
    def _():
        start(next_e)

    arrived(row_g1)
    shift(trans.at[0], g1, goff.at[0], pg)
    arrived(row_l1)
    times(trans.at[0], l1, mixed)
    arrived(row_e0)
    times_transposed(mixed, e0, spread.at[0], pl_own)

    @pl.when(gives_one)
    def _():
        start(next_g)

    @pl.when(gives_direct)
    def _():
        start(next_l)

    @pl.when(gives_relay)
    def _():
        start(relay_l)

    arrived(row_pe)

    @pl.when(takes_two)
    def _():
        arrived(far_e)
        start(row_fe)
        arrived(far_g)
        start(row_fg)

    @pl.when(takes_one)
    def _():
        arrived(next_e)
        start(row_ne)
        arrived(next_g)
        start(row_ng)
        arrived(row_ne)
        times(trans.at[1], ne, te.at[own, :])
        start(row_te)
        times(pe.at[own, :], ne, out_trans.at[0])
        arrived(row_ng)
        shift(trans.at[1], ng, goff.at[1], tg)
        shift(pe.at[own, :], ng, pg, out_goff.at[0])

    @pl.when(takes_two)
    def _():
        arrived(far_l)
        start(row_fl)

    @pl.when(forwards)
    def _():
        for copy, onward in zip(relay_l, forward_l):
            copy.wait_recv()
            onward.start()

    @pl.when(takes_two)
    def _():
        arrived(row_fe)
        times(te.at[own, :], fe, out_trans.at[1])
        arrived(row_fg)
        shift(te.at[own, :], fg, tg, out_goff.at[1])
        arrived(row_fl)
        mirror(fl, cores, rows, width)
        times(te.at[own, :], fl, mixed_far)

    @pl.when(takes_direct)
    def _():
        for copy, onward in zip(next_l, row_nl):
            copy.wait_recv()
            onward.start()

    @pl.when(takes_forward)
    def _():
        for copy, onward in zip(forward_l, row_nl):
            copy.wait_recv()
            onward.start()

    @pl.when(takes_one)
    def _():
        start(row_nl[len(half):])
        arrived(row_nl)
        mirror(nl, cores, rows, width)
        times(pe.at[own, :], nl, mixed)
        times_transposed(mixed, pe, pl_own, out_spread.at[0])
        times(trans.at[1], nl, mixed)
        times_transposed(mixed, e1, spread.at[1], tl_own)
        arrived(row_te)

    @pl.when(takes_two)
    def _():
        times_transposed(mixed_far, te, tl_own, out_spread.at[1])

    @pl.when(position == count - 2)
    def _():
        out_trans[1] = te[own, :]
        out_spread[1] = tl_own[...]
        out_goff[1] = tg[...]

    @pl.when(position == count - 1)
    def _():
        out_trans[0] = pe[own, :]
        out_spread[0] = pl_own[...]
        out_goff[0] = pg[...]
        out_trans[1] = trans[1]
        out_spread[1] = spread[1]
        out_goff[1] = goff[1]

    left(row_e1 + row_l1 + row_g1 + row_e0 + row_pe)

    @pl.when(gives_two)
    def _():
        left(far_e + far_g + far_l)

    @pl.when(gives_one)
    def _():
        left(next_e + next_g)

    @pl.when(gives_direct)
    def _():
        left(next_l)

    @pl.when(gives_relay)
    def _():
        left(relay_l)

    @pl.when(forwards)
    def _():
        left(forward_l)

    @pl.when(takes_two)
    def _():
        left(row_fe + row_fg + row_fl)

    @pl.when(takes_one)
    def _():
        left(row_ne + row_ng + row_nl + row_te)


def on_device(count, cores, trans, offset, spread):
    _, rows, width = trans.shape
    kind = trans.dtype
    goff = jnp.broadcast_to(offset[:, None, :], (2, LINES, rows))
    full = pltpu.VMEM((width, width), kind)
    part = pltpu.VMEM((rows, width), kind)
    lines = pltpu.VMEM((cores, LINES, rows), kind)
    line = pltpu.VMEM((LINES, rows), kind)
    n_copies = 20 + 20 * (cores - 1)
    vmem = pl.BlockSpec(memory_space=pltpu.VMEM)
    flops = 12 * 2 * rows * width * width
    a, b, c = pl.pallas_call(
        functools.partial(kernel, count, cores),
        out_shape=(
            jax.ShapeDtypeStruct(trans.shape, kind),
            jax.ShapeDtypeStruct(goff.shape, kind),
            jax.ShapeDtypeStruct(spread.shape, kind),
        ),
        in_specs=[vmem] * 3,
        out_specs=(vmem,) * 3,
        scratch_shapes=[full] * 9 + [part] * 5 + [lines] * 3 + [line] * 2
        + [pltpu.SemaphoreType.DMA((n_copies,)), pltpu.SemaphoreType.DMA((n_copies,))],
        compiler_params=pltpu.CompilerParams(
            collective_id=0, has_side_effects=True, vmem_limit_bytes=56 * 1024 * 1024
        ),
        cost_estimate=pl.CostEstimate(flops=flops, bytes_accessed=4 * trans.size * 2, transcendentals=0),
    )(trans, goff, spread)
    return a, b[:, 0, :], c


def solution(mesh):
    placed = (P("tm", "row", None), P("tm", "row"), P("tm", "row", None))
    body = functools.partial(on_device, mesh.shape["tm"], mesh.shape["row"])
    return jax.shard_map(body, mesh=mesh, in_specs=placed, out_specs=placed, check_vma=False)
```

```python
import functools
import jax
import jax.numpy as jnp
from jax import lax
from jax.experimental import pallas as pl
from jax.experimental.pallas import tpu as pltpu
from jax.sharding import PartitionSpec as P

MESH = pl.DeviceIdType.MESH
LINES = 16
TILE = 256


def pieces(core, cores, rows, width):
    if cores != 2 or rows % 256 or width != 2 * rows:
        return [(0, rows, 0, width)]
    q = rows // 2
    return [
        (0, q, core * (2 * q), 2 * q),
        (core * q, q, (2 + core) * q, q),
        (q, q, (1 - core) * q, 2 * q),
    ]


def mirror(matrix, cores, rows, width):
    if cores != 2 or rows % 256 or width != 2 * rows:
        return
    q = rows // 2
    for i, j in ((1, 0), (2, 0), (2, 1), (3, 2), (0, 3), (1, 3)):
        block = matrix[pl.ds(j * q, q), pl.ds(i * q, q)]
        matrix[pl.ds(i * q, q), pl.ds(j * q, q)] = block.T


def kernel(
    count, cores, trans, goff, spread, out_trans, out_goff, out_spread,
    e0, e1, l1, pe, ne, nl, fe, fl, te, mixed, mixed_far, relay, pl_own, tl_own, g1, ng, fg, pg, tg,
    send_sem, recv_sem,
):
    rows, width = trans.shape[1:]
    tile = min(TILE, width)
    position = lax.axis_index("tm")
    core = lax.axis_index("row")
    peers = [(k, lax.rem(core + k, cores)) for k in range(1, cores)]
    used = [0]

    barrier = pltpu.get_barrier_semaphore()
    expected = jnp.int32(cores - 1)
    for _, peer in peers:
        pl.semaphore_signal(barrier, inc=1, device_id={"row": peer}, device_id_type=MESH)
    quads = count % 4 == 0
    quarter = lax.rem(position, 4)
    for step in (-2, -1, 1, 2) + ((-3, 3) if quads else ()):
        there = jnp.logical_and(position + step >= 0, position + step < count)
        if step == -3:
            there = jnp.logical_and(there, quarter == 2)
        if step == 3:
            there = jnp.logical_and(there, quarter == 3)
        expected = expected + there.astype(jnp.int32)

        @pl.when(there)
        def _(step=step):
            pl.semaphore_signal(barrier, inc=1, device_id={"tm": position + step}, device_id_type=MESH)

    pl.semaphore_wait(barrier, expected)

    def remote(source, target, device):
        k = used[0]
        used[0] += 1
        return pltpu.make_async_remote_copy(
            src_ref=source, dst_ref=target, send_sem=send_sem.at[k], recv_sem=recv_sem.at[k],
            device_id=device, device_id_type=MESH,
        )

    def place(index, size):
        if isinstance(index, int):
            return pl.ds(index, size)
        return pl.ds(pl.multiple_of(index, 128), size)

    own = place(core * rows, rows)

    def spread_rows(matrix, parts, source=None):
        copies = []
        for row, n_rows, column, n_columns in parts:
            target = matrix.at[place(core * rows + row, n_rows), place(column, n_columns)]
            if source is None:
                origin = target
            else:
                origin = source.at[place(row, n_rows), place(column, n_columns)]
            copies.append((origin, target))
        return copies

    whole = [(0, rows, 0, width)]
    half = pieces(core, cores, rows, width)

    def to_device(pairs, device):
        return [remote(a, b, device) for a, b in pairs]

    def to_peers(pairs):
        return [remote(a, b, {"row": peer}) for _, peer in peers for a, b in pairs]

    def start(copies):
        for copy in copies:
            copy.start()

    def arrived(copies):
        for copy in copies:
            copy.wait_recv()

    def left(copies):
        for copy in copies:
            copy.wait_send()

    def times(a, b, out):
        @pl.loop(0, width // tile)
        def _(n):
            columns = pl.ds(pl.multiple_of(n * tile, tile), tile)
            out[:, columns] = jnp.dot(
                a[...], b[:, columns], preferred_element_type=jnp.float32
            ).astype(jnp.bfloat16)

    def times_transposed(a, b, added, out):
        @pl.loop(0, width // tile)
        def _(n):
            columns = pl.ds(pl.multiple_of(n * tile, tile), tile)
            value = lax.dot_general(
                a[...], b[columns, :], (((1,), (1,)), ((), ())), preferred_element_type=jnp.float32
            )
            out[:, columns] = (value + added[:, columns].astype(jnp.float32)).astype(jnp.bfloat16)

    def shift(a, g, added, out):
        total = added[...].astype(jnp.float32)
        for k in range(cores):
            total = total + lax.dot_general(
                g[k], a[:, pl.ds(k * rows, rows)], (((1,), (1,)), ((), ())),
                preferred_element_type=jnp.float32,
            )
        out[...] = total.astype(jnp.bfloat16)

    two = {"tm": position - 2}
    relay_at, forward_to = position - 2, position + 1
    if quads:
        relay_at = jnp.where(quarter == 0, position + 2, position - 2)
        forward_to = jnp.where(quarter == 0, position + 1, position - 3)
    one = {"tm": position - 1}
    row_e1 = to_peers(spread_rows(e1, whole, trans.at[1]))
    row_l1 = to_peers(spread_rows(l1, whole, spread.at[1]))
    row_g1 = to_peers([(goff.at[1], g1.at[core])])
    row_e0 = to_peers(spread_rows(e0, whole, trans.at[0]))
    far_e = to_device(spread_rows(fe, whole, trans.at[0]), two)
    far_l = to_device(spread_rows(fl, half, spread.at[0]), two)
    far_g = to_device([(goff.at[0], fg.at[core])], two)
    next_e = to_device(spread_rows(ne, whole, pe.at[own, :]), one)
    next_l = to_device(spread_rows(nl, half, pl_own), one)
    relay_l = to_device(
        [(pl_own.at[place(a, n), place(b, m)], relay.at[place(a, n), place(b, m)]) for a, n, b, m in half],
        {"tm": relay_at},
    )
    forward_l = to_device(spread_rows(nl, half, relay), {"tm": forward_to})
    next_g = to_device([(pg, ng.at[core])], one)
    row_pe = to_peers(spread_rows(pe, whole))
    row_fe = to_peers(spread_rows(fe, whole))
    row_fl = to_peers(spread_rows(fl, half))
    row_fg = to_peers([(fg.at[core], fg.at[core])])
    row_ne = to_peers(spread_rows(ne, whole))
    row_nl = to_peers(spread_rows(nl, half))
    row_ng = to_peers([(ng.at[core], ng.at[core])])
    row_te = to_peers(spread_rows(te, whole))

    gives_two = position >= 2
    gives_one = position >= 1
    takes_two = position + 2 < count
    takes_one = position + 1 < count
    even = lax.rem(position, 2) == 0
    gives_direct = jnp.logical_and(gives_one, jnp.logical_not(even))
    gives_relay = jnp.logical_and(gives_one, even)
    forwards = jnp.logical_and(takes_two, even)
    if quads:
        forwards = jnp.logical_or(quarter == 0, jnp.logical_and(quarter == 2, position > 2))
    takes_direct = jnp.logical_and(takes_one, even)
    takes_forward = jnp.logical_and(takes_one, jnp.logical_not(even))

    start(row_e1)

    @pl.when(gives_two)
    def _():
        start(far_e + far_g)

    start(row_g1 + row_l1 + row_e0)
    e1[own, :] = trans[1]
    l1[own, :] = spread[1]
    e0[own, :] = trans[0]
    g1[core] = goff[1]

    arrived(row_e1)
    times(trans.at[0], e1, pe.at[own, :])
    start(row_pe)

    @pl.when(gives_one)
    def _():
        start(next_e)

    arrived(row_g1)
    shift(trans.at[0], g1, goff.at[0], pg)
    arrived(row_l1)
    times(trans.at[0], l1, mixed)
    arrived(row_e0)
    times_transposed(mixed, e0, spread.at[0], pl_own)

    @pl.when(gives_one)
    def _():
        start(next_g)

    @pl.when(gives_direct)
    def _():
        start(next_l)

    @pl.when(gives_relay)
    def _():
        start(relay_l)

    @pl.when(gives_two)
    def _():
        start(far_l)

    arrived(row_pe)

    @pl.when(takes_two)
    def _():
        arrived(far_e)
        start(row_fe)
        arrived(far_g)
        start(row_fg)

    @pl.when(takes_one)
    def _():
        arrived(next_e)
        start(row_ne)
        arrived(next_g)
        start(row_ng)
        arrived(row_ne)
        times(trans.at[1], ne, te.at[own, :])
        start(row_te)
        times(pe.at[own, :], ne, out_trans.at[0])
        arrived(row_ng)
        shift(trans.at[1], ng, goff.at[1], tg)
        shift(pe.at[own, :], ng, pg, out_goff.at[0])

    @pl.when(forwards)
    def _():
        for copy, onward in zip(relay_l, forward_l):
            copy.wait_recv()
            onward.start()

    @pl.when(takes_two)
    def _():
        arrived(row_fe)
        times(te.at[own, :], fe, out_trans.at[1])
        arrived(row_fg)
        shift(te.at[own, :], fg, tg, out_goff.at[1])

    @pl.when(takes_direct)
    def _():
        for copy, onward in zip(next_l, row_nl):
            copy.wait_recv()
            onward.start()

    @pl.when(takes_forward)
    def _():
        for copy, onward in zip(forward_l, row_nl):
            copy.wait_recv()
            onward.start()

    @pl.when(takes_one)
    def _():
        start(row_nl[len(half):])
        arrived(row_nl)
        mirror(nl, cores, rows, width)
        times(pe.at[own, :], nl, mixed)
        times_transposed(mixed, pe, pl_own, out_spread.at[0])
        times(trans.at[1], nl, mixed)
        times_transposed(mixed, e1, spread.at[1], tl_own)
        arrived(row_te)

    @pl.when(takes_two)
    def _():
        for copy, onward in zip(far_l, row_fl):
            copy.wait_recv()
            onward.start()
        start(row_fl[len(half):])
        arrived(row_fl)
        mirror(fl, cores, rows, width)
        times(te.at[own, :], fl, mixed_far)
        times_transposed(mixed_far, te, tl_own, out_spread.at[1])

    @pl.when(position == count - 2)
    def _():
        out_trans[1] = te[own, :]
        out_spread[1] = tl_own[...]
        out_goff[1] = tg[...]

    @pl.when(position == count - 1)
    def _():
        out_trans[0] = pe[own, :]
        out_spread[0] = pl_own[...]
        out_goff[0] = pg[...]
        out_trans[1] = trans[1]
        out_spread[1] = spread[1]
        out_goff[1] = goff[1]

    left(row_e1 + row_l1 + row_g1 + row_e0 + row_pe)

    @pl.when(gives_two)
    def _():
        left(far_e + far_g + far_l)

    @pl.when(gives_one)
    def _():
        left(next_e + next_g)

    @pl.when(gives_direct)
    def _():
        left(next_l)

    @pl.when(gives_relay)
    def _():
        left(relay_l)

    @pl.when(forwards)
    def _():
        left(forward_l)

    @pl.when(takes_two)
    def _():
        left(row_fe + row_fg + row_fl)

    @pl.when(takes_one)
    def _():
        left(row_ne + row_ng + row_nl + row_te)


def on_device(count, cores, trans, offset, spread):
    _, rows, width = trans.shape
    kind = trans.dtype
    goff = jnp.broadcast_to(offset[:, None, :], (2, LINES, rows))
    full = pltpu.VMEM((width, width), kind)
    part = pltpu.VMEM((rows, width), kind)
    lines = pltpu.VMEM((cores, LINES, rows), kind)
    line = pltpu.VMEM((LINES, rows), kind)
    n_copies = 20 + 20 * (cores - 1)
    vmem = pl.BlockSpec(memory_space=pltpu.VMEM)
    flops = 12 * 2 * rows * width * width
    a, b, c = pl.pallas_call(
        functools.partial(kernel, count, cores),
        out_shape=(
            jax.ShapeDtypeStruct(trans.shape, kind),
            jax.ShapeDtypeStruct(goff.shape, kind),
            jax.ShapeDtypeStruct(spread.shape, kind),
        ),
        in_specs=[vmem] * 3,
        out_specs=(vmem,) * 3,
        scratch_shapes=[full] * 9 + [part] * 5 + [lines] * 3 + [line] * 2
        + [pltpu.SemaphoreType.DMA((n_copies,)), pltpu.SemaphoreType.DMA((n_copies,))],
        compiler_params=pltpu.CompilerParams(
            collective_id=0, has_side_effects=True, vmem_limit_bytes=56 * 1024 * 1024
        ),
        cost_estimate=pl.CostEstimate(flops=flops, bytes_accessed=4 * trans.size * 2, transcendentals=0),
    )(trans, goff, spread)
    return a, b[:, 0, :], c


def solution(mesh):
    placed = (P("tm", "row", None), P("tm", "row"), P("tm", "row", None))
    body = functools.partial(on_device, mesh.shape["tm"], mesh.shape["row"])
    return jax.shard_map(body, mesh=mesh, in_specs=placed, out_specs=placed, check_vma=False)
```
